512 devices in a mesh: dp: 32 (over x, y_lo, core), tensor: 16 (over y_hi, z).
Axes of the slice: x: 4, y: 8 (y_hi: 2, y_lo: 4; y = y_hi * 4 + y_lo), z: 8, core: 2. Of those that a mesh axis runs over, the one named last changes fastest.
Arguments:
- layer_input: bfloat16 [32768, 4096], P('dp', 'tensor'), may hold values from -6 to 6
- up_grad: bfloat16 [32768, 14336], P('dp', 'tensor'), may hold values from -6 to 6
- hidden: bfloat16 [32768, 14336], P('dp', 'tensor'), may hold values from -6 to 6
- down_grad: bfloat16 [32768, 4096], P('dp', 'tensor'), may hold values from -6 to 6
- first_in: bfloat16 [4096, 64], P('tensor'), may hold values from -0.09375 to 0.09375
- first_out: bfloat16 [14336, 64], P('tensor'), may hold values from -0.046875 to 0.046875
- second_in: bfloat16 [14336, 64], P('tensor'), may hold values from -0.046875 to 0.046875
- second_out: bfloat16 [4096, 64], P('tensor'), may hold values from -0.09375 to 0.09375
- queries: bfloat16 [512, 8192], P('dp', 'tensor'), may hold values from -0.0078125 to 0.0078125
Outputs:
- scores: float32 [512, 512], P(('dp', 'tensor'))
The draws below stay inside these ranges and needn't reach their ends.
All inputs are finite; a program needn't handle non-finite values.
Results may differ from the reference program's by a relative error of at most 0.014.
Values may be sent and summed in bfloat16 or wider, within the bound.
No kernel may reach another device: no remote copies, remote signals or barrier semaphores. Data moves between devices by JAX's collectives and lax.ppermute only.
A program may use at most 64 MiB of HBM per device.

```python
import jax
import jax.numpy as jnp
from jax import lax

D = 4096
FF = 14336
K = 64
LEN = 64
TRAIN = 512
QUERIES = 512
TOKENS = 32768


def steps_of(own_key, shape, cuts, least, largest):
    level, own = 1.0, jax.random.fold_in(own_key, 6)
    for axis_at, parts in cuts:
        draws = jnp.exp(jax.random.uniform(jax.random.fold_in(own, axis_at), (parts,), jnp.float32, least / len(cuts), largest / len(cuts)))
        level = level * jnp.repeat(draws, shape[axis_at] // parts).reshape([-1 if axis == axis_at else 1 for axis in range(len(shape))])
    return level


def normal_values(key, extent, spread, bound, cuts=(), held_as=jnp.bfloat16):
    drawn = jax.random.normal(key, extent, jnp.float32) * spread
    if len(cuts) > 0:
        drawn = steps_of(key, extent, cuts, -0.22, 0.18) * drawn
    return jnp.clip(drawn, min=-bound, max=bound).astype(held_as)


def setup_inputs(seed: int = 0) -> dict:
    key_list = jax.random.split(jax.random.key(seed), 10)
    layer_input = normal_values(key_list[0], (TOKENS, D), 1.0, 6.0, ((0, 32), (1, 16)))
    up_grad = normal_values(key_list[1], (TOKENS, FF), 1.0, 6.0, ((0, 32), (1, 16)))
    hidden = normal_values(key_list[2], (TOKENS, FF), 1.0, 6.0, ((0, 32), (1, 16)))
    down_grad = normal_values(key_list[3], (TOKENS, D), 1.0, 6.0, ((0, 32), (1, 16)))
    first_in = normal_values(key_list[4], (D, K), D ** -0.5, 0.09375, ((0, 16),))
    first_out = normal_values(key_list[5], (FF, K), FF ** -0.5, 0.046875, ((0, 16),))
    second_in = normal_values(key_list[6], (FF, K), FF ** -0.5, 0.046875, ((0, 16),))
    second_out = normal_values(key_list[7], (D, K), D ** -0.5, 0.09375, ((0, 16),))
    queries = normal_values(key_list[8], (QUERIES, 2 * K * K), (2 * K * K * LEN) ** -0.5, 0.0078125, ((0, 32), (1, 16)))
    return {"layer_input": layer_input, "up_grad": up_grad, "hidden": hidden, "down_grad": down_grad, "first_in": first_in, "first_out": first_out, "second_in": second_in, "second_out": second_out, "queries": queries}


def layer_sketch(grad_side, input_side):
    grad_side = grad_side.reshape(TRAIN, LEN, K)
    input_side = input_side.reshape(TRAIN, LEN, K)
    return jnp.einsum("sti,stj->sij", grad_side, input_side).reshape(TRAIN, K * K)


def reference(layer_input, up_grad, hidden, down_grad, first_in, first_out, second_in, second_out, queries):
    first_a = jnp.dot(layer_input, first_in, preferred_element_type=jnp.float32)
    first_b = jnp.dot(up_grad, first_out, preferred_element_type=jnp.float32)
    second_a = jnp.dot(hidden, second_in, preferred_element_type=jnp.float32)
    second_b = jnp.dot(down_grad, second_out, preferred_element_type=jnp.float32)
    sketch = jnp.concatenate([layer_sketch(first_b, first_a), layer_sketch(second_b, second_a)], axis=1).astype(jnp.bfloat16)
    return lax.dot_general(sketch, queries, (((1,), (1,)), ((), ())), preferred_element_type=jnp.float32)
```

```python
import jax
import jax.numpy as jnp
from jax import lax
from jax.sharding import PartitionSpec as P

K = 64
LEN = 64
T = ("yh", "z")
D = ("x", "yl", "c")


def local(
    layer_input, up_grad, hidden, down_grad, first_in, first_out, second_in, second_out, queries
):
    rows, width = queries.shape
    copies = jnp.broadcast_to(queries[None], (8, rows, width))
    q = lax.all_to_all(copies, ("yh", "yl"), 0, 0, tiled=True).reshape(2, 4, rows, width)
    pieces = [
        jnp.dot(x, w, preferred_element_type=jnp.float32).astype(jnp.bfloat16)
        for x, w in (
            (layer_input, first_in),
            (up_grad, first_out),
            (hidden, second_in),
            (down_grad, second_out),
        )
    ]
    projected = jnp.concatenate(pieces, axis=1).reshape(16, LEN, 4 * K)
    projected, q = lax.optimization_barrier((projected, q))
    shares = lax.all_to_all(projected, T, 0, 0, tiled=True)
    q = lax.all_gather(q, "x", axis=0)
    halves = [lax.all_gather(q[:, h], "c", axis=0).reshape(32 * rows, width) for h in range(2)]
    p = jnp.sum(shares.astype(jnp.float32), axis=0)
    sketch = jnp.stack(
        [
            lax.dot_general(b, a, (((0,), (0,)), ((), ())), preferred_element_type=jnp.float32)
            .astype(jnp.bfloat16)
            .reshape(8, width)
            for a, b in (
                (p[:, 0:K], p[:, K : 2 * K]),
                (p[:, 2 * K : 3 * K], p[:, 3 * K :]),
            )
        ],
        axis=1,
    )
    sketch = lax.all_to_all(sketch, "z", 0, 0, tiled=True)
    part = sum(
        lax.dot_general(
            sketch[:, h], halves[h], (((1,), (1,)), ((), ())), preferred_element_type=jnp.float32
        )
        for h in range(2)
    )
    part = lax.all_to_all(part, "z", 0, 0, tiled=True)
    row = jnp.sum(part, axis=0).reshape(2, 16, rows)
    return jnp.transpose(row, (1, 0, 2)).reshape(1, 32 * rows)


def solution(mesh):
    fine = jax.sharding.Mesh(mesh.devices.reshape(4, 4, 2, 2, 8), D + T)
    placed = (P(D, T),) * 4 + (P(T, None),) * 4 + (P(D, T),)
    return jax.shard_map(
        local, mesh=fine, in_specs=placed, out_specs=P(D + T, None), check_vma=False
    )
```

```python
import jax
import jax.numpy as jnp
from jax import lax
from jax.experimental import pallas as pl
from jax.experimental.pallas import tpu as pltpu
from jax.sharding import PartitionSpec as P

K = 64
LEN = 64
T = ("yh", "z")
D = ("x", "yl", "c")
WHOLE = pl.BlockSpec(memory_space=pltpu.VMEM)
F32 = jnp.float32
BF16 = jnp.bfloat16


def project_kernel(x0, x1, x2, x3, w0, w1, w2, w3, out):
    def layer(xa, xb, wa, wb):
        x = jnp.concatenate([xa[...], xb[...]], axis=1)
        w = jnp.concatenate(
            [
                jnp.concatenate([wa[...], jnp.zeros(wb.shape, BF16)], axis=1),
                jnp.concatenate([jnp.zeros(wa.shape, BF16), wb[...]], axis=1),
            ],
            axis=0,
        )
        return lax.dot_general(x, w, (((1,), (1,)), ((), ())), preferred_element_type=F32)

    both = jnp.concatenate([layer(x0, x1, w0, w1), layer(x2, x3, w2, w3)], axis=1)
    out[...] = both.astype(BF16).reshape(out.shape)


def project(xs, ws):
    rows = 512
    xs = [pltpu.with_memory_space_constraint(x, pltpu.HBM) for x in xs]
    ws = [pltpu.with_memory_space_constraint(w.T, pltpu.HBM) for w in ws]
    return pl.pallas_call(
        project_kernel,
        out_shape=jax.ShapeDtypeStruct((16, LEN, 4 * K), BF16),
        grid=(xs[0].shape[0] // rows,),
        in_specs=[pl.BlockSpec((rows, x.shape[1]), lambda i: (i, 0)) for x in xs]
        + [pl.BlockSpec(w.shape, lambda i: (0, 0)) for w in ws],
        out_specs=pl.BlockSpec((rows // LEN, LEN, 4 * K), lambda i: (i, 0, 0)),
        compiler_params=pltpu.CompilerParams(vmem_limit_bytes=40 << 20),
        name="project",
    )(*xs, *ws)


def sketches(shares):
    p = jnp.sum(shares.astype(F32), axis=0)
    return jnp.stack(
        [
            lax.dot_general(p[:, s + K : s + 2 * K], p[:, s : s + K], (((0,), (0,)), ((), ())), preferred_element_type=F32)
            .astype(BF16)
            .reshape(8, 8 * K)
            for s in (0, 2 * K)
        ],
        axis=1,
    )


def score_kernel(sketch, *refs):
    pieces, out = refs[:-1], refs[-1]
    me = lax.axis_index("x")
    for k, piece in enumerate(pieces):
        total = None
        for l in range(2):
            rows = jnp.concatenate([piece[c, l, y] for y in range(4) for c in range(2)], axis=0)
            part = lax.dot_general(sketch[:, l, :], rows, (((1,), (1,)), ((), ())), preferred_element_type=F32)
            total = part if total is None else total + part
        at = lax.rem(me + 4 - k, 4) * 128
        out[:, pl.ds(pl.multiple_of(at, 128), 128)] = total


def score(sketch, pieces):
    return pl.pallas_call(
        score_kernel,
        out_shape=jax.ShapeDtypeStruct((8, 512), F32),
        in_specs=[WHOLE] * (1 + len(pieces)),
        out_specs=WHOLE,
        compiler_params=pltpu.CompilerParams(vmem_limit_bytes=16 << 20),
        name="score",
    )(sketch, *pieces)


def local(layer_input, up_grad, hidden, down_grad, first_in, first_out, second_in, second_out, queries):
    rows, width = queries.shape
    copies = jnp.broadcast_to(queries[None], (8, rows, width))
    q = lax.all_to_all(copies, ("yh", "yl"), 0, 0, tiled=True).reshape(2, 4, rows, width)
    projected = project((layer_input, up_grad, hidden, down_grad), (first_in, first_out, second_in, second_out))
    projected, q = lax.optimization_barrier((projected, q))
    shares = lax.all_to_all(projected, T, 0, 0, tiled=True)
    q = lax.all_gather(q, "c", axis=0)
    pieces = [q] + [lax.ppermute(q, "x", [(i, (i + k) % 4) for i in range(4)]) for k in (1, 3, 2)]
    pieces = [pieces[0], pieces[1], pieces[3], pieces[2]]
    sketch = lax.all_to_all(sketches(shares), "z", 0, 0, tiled=True)
    part = score(sketch, pieces)
    part = lax.all_to_all(part, "z", 0, 0, tiled=True)
    return jnp.sum(part, axis=0, keepdims=True)


def solution(mesh):
    fine = jax.sharding.Mesh(mesh.devices.reshape(4, 4, 2, 2, 8), D + T)
    placed = (P(D, T),) * 4 + (P(T, None),) * 4 + (P(D, T),)
    return jax.shard_map(local, mesh=fine, in_specs=placed, out_specs=P(D + T, None), check_vma=False)
```

```python
import jax
import jax.numpy as jnp
from jax import lax
from jax.experimental import pallas as pl
from jax.experimental.pallas import tpu as pltpu
from jax.sharding import PartitionSpec as P

K = 64
LEN = 64
T = ("yh", "z")
D = ("x", "yl", "c")
WHOLE = pl.BlockSpec(memory_space=pltpu.VMEM)
F32 = jnp.float32
BF16 = jnp.bfloat16


def project_kernel(x0, x1, x2, x3, w0, w1, w2, w3, out):
    def layer(xa, xb, wa, wb):
        x = jnp.concatenate([xa[...], xb[...]], axis=1)
        w = jnp.concatenate(
            [
                jnp.concatenate([wa[...], jnp.zeros(wb.shape, BF16)], axis=1),
                jnp.concatenate([jnp.zeros(wa.shape, BF16), wb[...]], axis=1),
            ],
            axis=0,
        )
        return lax.dot_general(x, w, (((1,), (1,)), ((), ())), preferred_element_type=F32)

    both = jnp.concatenate([layer(x0, x1, w0, w1), layer(x2, x3, w2, w3)], axis=1)
    out[...] = both.astype(BF16).reshape(out.shape)


def project(xs, ws):
    rows = 512
    xs = [pltpu.with_memory_space_constraint(x, pltpu.HBM) for x in xs]
    ws = [pltpu.with_memory_space_constraint(w.T, pltpu.HBM) for w in ws]
    return pl.pallas_call(
        project_kernel,
        out_shape=jax.ShapeDtypeStruct((16, LEN, 4 * K), BF16),
        grid=(xs[0].shape[0] // rows,),
        in_specs=[pl.BlockSpec((rows, x.shape[1]), lambda i: (i, 0)) for x in xs]
        + [pl.BlockSpec(w.shape, lambda i: (0, 0)) for w in ws],
        out_specs=pl.BlockSpec((rows // LEN, LEN, 4 * K), lambda i: (i, 0, 0)),
        compiler_params=pltpu.CompilerParams(vmem_limit_bytes=40 << 20),
        name="project",
    )(*xs, *ws)


def sketches(shares):
    p = jnp.sum(shares.astype(F32), axis=0)
    return jnp.stack(
        [
            lax.dot_general(p[:, s + K : s + 2 * K], p[:, s : s + K], (((0,), (0,)), ((), ())), preferred_element_type=F32)
            .astype(BF16)
            .reshape(8, 8 * K)
            for s in (0, 2 * K)
        ],
        axis=1,
    )


def score_kernel(sketch, *refs):
    pieces, out = refs[:-1], refs[-1]
    me = lax.axis_index("x")
    totals = []
    for piece in pieces:
        total = None
        for l in range(2):
            rows = jnp.concatenate([piece[l, y] for y in range(4)], axis=0)
            part = lax.dot_general(sketch[:, l, :], rows, (((1,), (1,)), ((), ())), preferred_element_type=F32)
            total = part if total is None else total + part
        totals.append(total)
    slots = []
    for x in range(4):
        away = lax.rem(me + 4 - x, 4)
        slot = totals[3]
        for k in range(3):
            slot = jnp.where(away == k, totals[k], slot)
        slots.append(slot)
    out[...] = jnp.concatenate(slots, axis=1)


def score(sketch, pieces):
    return pl.pallas_call(
        score_kernel,
        out_shape=jax.ShapeDtypeStruct((16, 256), F32),
        in_specs=[WHOLE] * (1 + len(pieces)),
        out_specs=WHOLE,
        compiler_params=pltpu.CompilerParams(vmem_limit_bytes=16 << 20),
        name="score",
    )(sketch, *pieces)


def local(layer_input, up_grad, hidden, down_grad, first_in, first_out, second_in, second_out, queries):
    rows, width = queries.shape
    copies = jnp.broadcast_to(queries[None], (8, rows, width))
    q = lax.all_to_all(copies, ("yh", "yl"), 0, 0, tiled=True).reshape(2, 4, rows, width)
    projected = project((layer_input, up_grad, hidden, down_grad), (first_in, first_out, second_in, second_out))
    projected, q = lax.optimization_barrier((projected, q))
    shares = lax.all_to_all(projected, T, 0, 0, tiled=True)
    pieces = [q] + [lax.ppermute(q, "x", [(i, (i + k) % 4) for i in range(4)]) for k in (1, 3, 2)]
    pieces = [pieces[0], pieces[1], pieces[3], pieces[2]]
    sketch = sketches(shares)
    sketch = jnp.concatenate([sketch, sketch], axis=0)
    sketch = lax.all_to_all(sketch, ("c", "z"), 0, 0, tiled=True)
    part = score(sketch, pieces)
    part = lax.all_to_all(part, ("c", "z"), 0, 0, tiled=True)
    row = jnp.sum(part.reshape(2, 8, 256), axis=1)
    return jnp.transpose(row.reshape(2, 16, rows), (1, 0, 2)).reshape(1, 32 * rows)


def solution(mesh):
    fine = jax.sharding.Mesh(mesh.devices.reshape(4, 4, 2, 2, 8), D + T)
    placed = (P(D, T),) * 4 + (P(T, None),) * 4 + (P(D, T),)
    return jax.shard_map(local, mesh=fine, in_specs=placed, out_specs=P(D + T, None), check_vma=False)
```

```python
import jax
import jax.numpy as jnp
from jax import lax
from jax.experimental import pallas as pl
from jax.experimental.pallas import tpu as pltpu
from jax.sharding import PartitionSpec as P

K = 64
LEN = 64
T = ("yh", "z")
D = ("x", "yl", "c")
WHOLE = pl.BlockSpec(memory_space=pltpu.VMEM)
F32 = jnp.float32
BF16 = jnp.bfloat16


def project_kernel(x0, x1, x2, x3, w0, w1, w2, w3, out):
    def layer(xa, xb, wa, wb):
        x = jnp.concatenate([xa[...], xb[...]], axis=1)
        w = jnp.concatenate(
            [
                jnp.concatenate([wa[...], jnp.zeros(wb.shape, BF16)], axis=1),
                jnp.concatenate([jnp.zeros(wa.shape, BF16), wb[...]], axis=1),
            ],
            axis=0,
        )
        return lax.dot_general(x, w, (((1,), (1,)), ((), ())), preferred_element_type=F32)

    both = jnp.concatenate([layer(x0, x1, w0, w1), layer(x2, x3, w2, w3)], axis=1)
    out[...] = both.astype(BF16).reshape(out.shape)


def project(xs, ws):
    rows = 512
    xs = [pltpu.with_memory_space_constraint(x, pltpu.HBM) for x in xs]
    ws = [pltpu.with_memory_space_constraint(w.T, pltpu.HBM) for w in ws]
    return pl.pallas_call(
        project_kernel,
        out_shape=jax.ShapeDtypeStruct((16, LEN, 4 * K), BF16),
        grid=(xs[0].shape[0] // rows,),
        in_specs=[pl.BlockSpec((rows, x.shape[1]), lambda i: (i, 0)) for x in xs]
        + [pl.BlockSpec(w.shape, lambda i: (0, 0)) for w in ws],
        out_specs=pl.BlockSpec((rows // LEN, LEN, 4 * K), lambda i: (i, 0, 0)),
        compiler_params=pltpu.CompilerParams(vmem_limit_bytes=40 << 20),
        name="project",
    )(*xs, *ws)


def sketches(shares):
    p = jnp.sum(shares.astype(F32), axis=0)
    return jnp.stack(
        [
            lax.dot_general(p[:, s + K : s + 2 * K], p[:, s : s + K], (((0,), (0,)), ((), ())), preferred_element_type=F32)
            .astype(BF16)
            .reshape(8, 8 * K)
            for s in (0, 2 * K)
        ],
        axis=1,
    )


def score_kernel(sketch, q, out):
    slots = []
    for x in range(4):
        total = None
        for l in range(2):
            rows = jnp.concatenate([q[x, l, y] for y in range(4)], axis=0)
            part = lax.dot_general(sketch[:, l, :], rows, (((1,), (1,)), ((), ())), preferred_element_type=F32)
            total = part if total is None else total + part
        slots.append(total)
    out[...] = jnp.concatenate(slots, axis=1)


def score(sketch, pieces):
    return pl.pallas_call(
        score_kernel,
        out_shape=jax.ShapeDtypeStruct((16, 256), F32),
        in_specs=[WHOLE] * (1 + len(pieces)),
        out_specs=WHOLE,
        compiler_params=pltpu.CompilerParams(vmem_limit_bytes=16 << 20),
        name="score",
    )(sketch, *pieces)


def local(layer_input, up_grad, hidden, down_grad, first_in, first_out, second_in, second_out, queries):
    rows, width = queries.shape
    copies = jnp.broadcast_to(queries[None], (8, rows, width))
    q = lax.all_to_all(copies, ("yh", "yl"), 0, 0, tiled=True).reshape(2, 4, rows, width)
    projected = project((layer_input, up_grad, hidden, down_grad), (first_in, first_out, second_in, second_out))
    projected, q = lax.optimization_barrier((projected, q))
    shares = lax.all_to_all(projected, T, 0, 0, tiled=True)
    pieces = [lax.all_gather(q, "x", axis=0)]
    shares, pieces = lax.optimization_barrier((shares, pieces))
    sketch = sketches(shares)
    sketch = jnp.concatenate([sketch, sketch], axis=0)
    sketch = lax.all_to_all(sketch, ("c", "z"), 0, 0, tiled=True)
    part = score(sketch, pieces)
    part = lax.all_to_all(part, ("c", "z"), 0, 0, tiled=True)
    row = jnp.sum(part.reshape(2, 8, 256), axis=1)
    return jnp.transpose(row.reshape(2, 16, rows), (1, 0, 2)).reshape(1, 32 * rows)


def solution(mesh):
    fine = jax.sharding.Mesh(mesh.devices.reshape(4, 4, 2, 2, 8), D + T)
    placed = (P(D, T),) * 4 + (P(T, None),) * 4 + (P(D, T),)
    return jax.shard_map(local, mesh=fine, in_specs=placed, out_specs=P(D + T, None), check_vma=False)
```
